128 devices in a mesh: group: 8 (over y, core), dp: 16 (over x, z).
Axes of the slice: x: 4, y: 4, z: 4, core: 2. Of those that a mesh axis runs over, the one named last changes fastest.
Arguments:
- acts: bfloat16 [131072, 2048], P(('group', 'dp')), may hold values from -6 to 6
- grad_out: bfloat16 [131072, 2048], P(('group', 'dp')), may hold values from -0.1875 to 0.1875
- error_in: bfloat16 [262144, 2048], P(('group', 'dp')), may hold values from -6 to 6
- kept: int32 [128, 328], P(('group', 'dp')), may hold values from 0 to 32767, as said below
- bounds: int32 [17], replicated, may hold values from 0 to 32768, as said below
Outputs:
- new_error: bfloat16 [262144, 2048], P(('group', 'dp'))
- regathered: float32 [128, 328, 128], P(('group', 'dp'))
The draws below stay inside these ranges and needn't reach their ends.
Inputs may be any that keep to these rules, and one draw needn't show every extreme that they name: `kept`: row d lists 328 different block numbers in no particular order. In each group one region (drawn per group) holds exactly 80 of every device's blocks; each device's other blocks lie in the other regions with counts that differ by at most one. bounds[0] = 0 and bounds[16] = 32768; every region holds at least 1024 blocks and at most 3072, and some region exactly 3072.
All inputs are finite; a program needn't handle non-finite values.
Results may differ from the reference program's by a relative error of at most 0.001.
Values sent between devices are 32-bit elements; how exact they have to be, the bound alone decides.
A program may use at most 128 MiB of HBM per device.

```python
import jax
import jax.numpy as jnp
from jax import lax

D = 2048
BLK = 128
TOK_DEV = 1024
KEEP = 328
CAP = 80
TOKENS = 131072
NB = 32768
REGMAX = 3072
N_GROUP = 8
N_DP = 16
DEVICES = 128


def region_layout(key):
    base = NB // N_DP
    quarter = base // 4
    key_delta, key_wide = jax.random.split(jax.random.fold_in(key, 11))
    delta = jax.random.randint(key_delta, (N_DP,), -quarter, quarter + 1)
    wide = jax.random.randint(key_wide, (), 0, N_DP)
    owners = jnp.arange(N_DP)
    delta = jnp.where(owners == wide, quarter, delta)
    delta = jnp.where(owners == (wide - 1) % N_DP, -quarter, delta)
    widths = base + delta - jnp.roll(delta, 1)
    bounds = jnp.concatenate([jnp.zeros((1,), jnp.int32), jnp.cumsum(widths).astype(jnp.int32)])
    return (bounds.astype(jnp.int32), widths.astype(jnp.int32))


def draw_bounds(key, part):
    bounds, widths = region_layout(key)
    return bounds


def draw_kept(key, part):
    bounds, widths = region_layout(key)
    key = jax.random.fold_in(key, 3)
    key_hot, key_order, key_rot, key_mix = jax.random.split(key, 4)
    hot = jax.random.randint(key_hot, (N_GROUP,), 0, N_DP)
    device_hot = jnp.repeat(hot, N_DP)
    rot = jax.random.randint(key_rot, (DEVICES,), 0, N_DP - 1)
    spread = KEEP - CAP
    each = spread // (N_DP - 1)
    extra = spread % (N_DP - 1)
    owners = jnp.arange(N_DP)
    relative = (owners[None, :] - device_hot[:, None] - 1) % N_DP
    shifted = (relative - rot[:, None]) % (N_DP - 1)
    counts = jnp.where(relative == N_DP - 1, CAP, each + (shifted < extra).astype(jnp.int32))
    scores = jax.random.randint(key_order, (DEVICES, N_DP, REGMAX), 0, 2 ** 29)
    spots = jnp.arange(REGMAX)
    scores = scores + jnp.where(spots[None, None, :] >= widths[None, :, None], 2 ** 30, 0)
    order = jnp.argsort(scores, axis=-1, stable=True)[:, :, :CAP]
    candidates = (bounds[:-1][None, :, None] + order).reshape(DEVICES, N_DP * CAP)
    live = (jnp.arange(CAP)[None, None, :] < counts[:, :, None]).reshape(DEVICES, N_DP * CAP)
    mixing = jax.random.randint(key_mix, (DEVICES, N_DP * CAP), 0, 2 ** 29)
    mixing = mixing + jnp.where(live, 0, 2 ** 30)
    pick = jnp.argsort(mixing, axis=-1, stable=True)[:, :KEEP]
    return jnp.take_along_axis(candidates, pick, axis=1).astype(jnp.int32)


def level_of(stream_key, shape, pieces, least, largest):
    factor_of, own = 1.0, jax.random.fold_in(stream_key, 6)
    for position, shards_of in pieces:
        heights = jnp.exp(jax.random.uniform(jax.random.fold_in(own, position), (shards_of,), jnp.float32, least / len(pieces), largest / len(pieces)))
        factor_of = factor_of * jnp.repeat(heights, shape[position] // shards_of).reshape([-1 if axis == position else 1 for axis in range(len(shape))])
    return factor_of


def centred(rng, extent, width, bound, cuts=(), kind=jnp.bfloat16):
    values = width * jax.random.normal(rng, extent, jnp.float32)
    if cuts:
        values = values * level_of(rng, extent, cuts, -0.22, 0.18)
    return jnp.clip(values, -bound, bound).astype(kind)


def setup_inputs(seed: int = 0) -> dict:
    streams_of = jax.random.split(jax.random.key(seed), 6)
    acts = centred(streams_of[0], (TOKENS, D), 1.0, 6.0, ((0, 128),))
    grad_out = centred(streams_of[1], (TOKENS, D), TOK_DEV ** -0.5, 0.1875, ((0, 128),))
    error_in = centred(streams_of[2], (DEVICES * D, D), 1.0, 6.0, ((0, 128),))
    kept = draw_kept(jax.random.fold_in(streams_of[5], 71), 0)
    bounds = draw_bounds(jax.random.fold_in(streams_of[5], 71), 0)
    return {"acts": acts, "grad_out": grad_out, "error_in": error_in, "kept": kept, "bounds": bounds}


def reference(acts, grad_out, error_in, kept, bounds):

    def device_step(summed, index):
        xs = lax.dynamic_slice_in_dim(acts, index * TOK_DEV, TOK_DEV, 0).astype(jnp.float32)
        dys = lax.dynamic_slice_in_dim(grad_out, index * TOK_DEV, TOK_DEV, 0).astype(jnp.float32)
        errs = lax.dynamic_slice_in_dim(error_in, index * D, D, 0).astype(jnp.float32)
        acc = jnp.dot(xs.T, dys, precision=lax.Precision.HIGHEST) + errs
        blocks = acc.reshape(NB, BLK)
        ids = kept[index]
        summed = summed.at[ids].add(blocks[ids])
        cleared = blocks.at[ids].set(0.0).reshape(D, D).astype(jnp.bfloat16)
        return (summed, cleared)
    start = jnp.zeros((NB, BLK), jnp.float32)
    summed, cleared = lax.scan(device_step, start, jnp.arange(DEVICES, dtype=jnp.int32))
    numbers = jnp.arange(NB, dtype=jnp.int32)
    region_of = lax.optimization_barrier(jnp.sum((numbers[:, None] >= bounds[None, 1:N_DP]).astype(jnp.int32), axis=1))
    region_sq = jax.ops.segment_sum(lax.optimization_barrier(jnp.sum(summed * summed, axis=1)), region_of, N_DP)
    widths = (bounds[1:] - bounds[:-1]).astype(jnp.float32)
    region_rms = jnp.sqrt(region_sq / (widths * BLK) + 1e-06)
    scaled = summed / region_rms[region_of][:, None]
    return (cleared.reshape(DEVICES * D, D), scaled[kept])
```

```python
import functools

import jax
import jax.numpy as jnp
from jax import lax
from jax.experimental import pallas as pl
from jax.experimental.pallas import tpu as pltpu
from jax.sharding import PartitionSpec as P

MESH = pl.DeviceIdType.MESH
CAP = 80
SUB = 8
ROWS = CAP // SUB
LANES = 128
WIDE = LANES // SUB
F32, BF16, I32 = jnp.float32, jnp.bfloat16, jnp.int32


def iota(shape, dim):
    return lax.broadcasted_iota(I32, shape, dim)


def onehot(mask):
    return jnp.where(mask, 1.0, 0.0).astype(BF16)


def dot(a, b, ca, cb):
    return lax.dot_general(a, b, (((ca,), (cb,)), ((), ())), preferred_element_type=F32)


def split(x):
    hi = x.astype(BF16)
    return hi, (x - hi.astype(F32)).astype(BF16)


def swap_blocks(x):
    n = x.shape[0]
    row = iota(x.shape, 0) & 7
    blk = iota(x.shape, 1) // WIDE
    for k in (1, 2, 4):
        low_row = (row & k) == 0
        low_blk = (blk & k) == 0
        up = pltpu.roll(pltpu.roll(x, n - k, 0), k * WIDE, 1)
        down = pltpu.roll(pltpu.roll(x, k, 0), LANES - k * WIDE, 1)
        x = jnp.where(low_row == low_blk, x, jnp.where(low_row, up, down))
    return x


def grads_kernel(
    keep, owners, acts, grad, err, kept_v, kept_s, bounds, out, send, pos_out, acc, ids_s, vals
):
    step = pl.program_id(0)
    steps = pl.num_programs(0)
    tile, width = err.shape
    pad = ids_s.shape[1]
    per_row = width // LANES

    @pl.when(step == 0)
    def _():
        ids_s[...] = jnp.full(ids_s.shape, -1, I32)
        ids_s[0:1, 0:keep] = kept_v[...]
        vals[...] = jnp.zeros(vals.shape, F32)

    ids = ids_s[0:1, :]
    live = ids >= 0
    full = dot(acts[...], grad[...], 0, 0) + err[...].astype(F32)
    hit_row = onehot((iota((tile, pad), 0) + step * tile == ids // per_row) & live)
    hit_col = onehot((iota((LANES, pad), 0) == ids % per_row) & live)
    cleared = dot(hit_row, hit_col, 1, 1)
    for c in range(per_row):
        block = full[:, c * LANES : (c + 1) * LANES]
        acc[c, pl.ds(step * tile, tile), :] = block
        out[:, c * LANES : (c + 1) * LANES] = jnp.where(
            cleared[:, c : c + 1] > 0.5, 0.0, block
        ).astype(BF16)

    @pl.when(step == steps - 1)
    def _():
        def take(k, carry):
            b = kept_s[0, k]
            vals[pl.ds(k, 1), :] = acc[b % per_row, pl.ds(b // per_row, 1), :]
            return carry

        lax.fori_loop(0, keep, take, 0, unroll=8)
        region = jnp.zeros(ids.shape, I32)
        for q in range(1, owners):
            region = region + (ids >= bounds[q]).astype(I32)
        of = (iota((owners, pad), 0) == region) & live
        earlier = onehot(iota((pad, pad), 0) < iota((pad, pad), 1))
        before = dot(onehot(of), earlier, 1, 0)
        slot = jnp.sum(jnp.where(of, before, 0.0), axis=0, keepdims=True).astype(I32)
        pos = jnp.where(live, region * CAP + slot, -1)
        pos_out[...] = jnp.broadcast_to(pos, pos_out.shape)
        at = onehot((iota((LANES, pad), 0) == slot) & live)
        high = jnp.where(of, (ids // 256).astype(F32), 0.0).astype(BF16)
        low = jnp.where(of, (ids % 256).astype(F32), 0.0).astype(BF16)
        number = dot(high, at, 1, 1) * 256.0 + dot(low, at, 1, 1)
        number = jnp.where(dot(onehot(of), at, 1, 1) > 0.5, number, -1048576.0)
        place = onehot((iota((owners * CAP, pad), 0) == pos) & live)
        hi, lo = split(vals[...])
        packed = swap_blocks(dot(place, hi, 1, 0) + dot(place, lo, 1, 0))
        for r in range(owners):
            for i in range(ROWS):
                tile_at = (r * ROWS + i) * SUB
                send[i, r * SUB : (r + 1) * SUB, :] = packed[tile_at : tile_at + SUB]
            send[ROWS, r * SUB : (r + 1) * SUB, :] = jnp.broadcast_to(
                number[r : r + 1, :], (SUB, LANES)
            )


def sums_kernel(groups, owners, bounds, send, back, got, oh, ans, ct, total, sems, bsem):
    g = lax.axis_index("group")
    d = lax.axis_index("dp")
    n = groups * owners
    me = g * owners + d
    home = d * groups + g
    heights = oh.shape[1]

    barrier = pltpu.get_barrier_semaphore()
    for i in range(1, groups):
        pl.semaphore_signal(
            barrier, inc=1, device_id=(lax.rem(g + i, groups), d), device_id_type=MESH
        )
    for i in range(1, owners):
        pl.semaphore_signal(
            barrier, inc=1, device_id=(g, lax.rem(d + i, owners)), device_id_type=MESH
        )
    pl.semaphore_wait(barrier, groups + owners - 2)
    for i in range(1, groups):
        pl.semaphore_signal(
            bsem, inc=1, device_id=(lax.rem(g + i, groups), d), device_id_type=MESH
        )
    pl.semaphore_wait(bsem, groups - 1)

    own = pltpu.make_async_copy(send.at[:, home, :], got.at[:, me, :], sems.at[4])
    own.start()

    def push(i, carry):
        tg = lax.rem(g + i // owners, groups)
        td = lax.rem(d + i % owners, owners)
        pltpu.make_async_remote_copy(
            src_ref=send.at[:, td * groups + tg, :],
            dst_ref=got.at[:, me, :],
            send_sem=sems.at[0],
            recv_sem=sems.at[1],
            device_id=(tg, td),
            device_id_type=MESH,
        ).start()
        return carry

    lax.fori_loop(1, n, push, 0)
    own.wait()
    most = got.at[:, pl.ds(0, n - 1), :]
    pltpu.make_async_copy(most, most, sems.at[1]).wait()
    pltpu.make_async_copy(most, most, sems.at[0]).wait()

    local = got[ROWS].T.astype(I32) - bounds[d]
    ct[0] = local >> 3
    ct[1] = local & 7
    total[...] = jnp.zeros(total.shape, F32)

    def add(i, carry):
        x = got[i].T
        hi = x.astype(BF16)
        hi, lo = hi.astype(F32), x - hi.astype(F32)
        high = ct[0, pl.ds(pl.multiple_of(i * SUB, SUB), SUB), :]
        low = ct[1, pl.ds(pl.multiple_of(i * SUB, SUB), SUB), :]
        parts = []
        for j in range(SUB):
            oh[i, :, j * n : (j + 1) * n] = onehot(iota((heights, n), 0) == high[j : j + 1, :])
            mine = [low[j : j + 1, :] == c for c in range(SUB)]
            rows = slice(j * WIDE, (j + 1) * WIDE)
            parts.append(
                jnp.concatenate(
                    [jnp.where(m, hi[rows], 0.0).astype(BF16) for m in mine]
                    + [jnp.where(m, lo[rows], 0.0).astype(BF16) for m in mine],
                    axis=0,
                )
            )
        total[...] += dot(oh[i], jnp.concatenate(parts, axis=1), 1, 1)
        return carry

    lax.fori_loop(0, ROWS, add, 0)
    whole = total[:, :LANES] + total[:, LANES:]
    ans[ROWS] = jnp.broadcast_to(jnp.sum(whole * whole, keepdims=True), (n, LANES))
    hi, lo = split(whole.T)
    table = jnp.concatenate([hi, lo], axis=0)

    def look(i, carry):
        both = dot(table, oh[i], 1, 0)
        both = both[:LANES] + both[LANES:]
        low = ct[1, pl.ds(pl.multiple_of(i * SUB, SUB), SUB), :]
        parts = []
        for j in range(SUB):
            picked = jnp.zeros((WIDE, n), F32)
            for c in range(SUB):
                picked = jnp.where(
                    low[j : j + 1, :] == c,
                    both[c * WIDE : (c + 1) * WIDE, j * n : (j + 1) * n],
                    picked,
                )
            parts.append(picked)
        ans[i] = jnp.concatenate(parts, axis=0).T
        return carry

    lax.fori_loop(0, ROWS, look, 0)

    own = pltpu.make_async_copy(ans.at[:, me, :], back.at[:, home, :], sems.at[4])
    own.start()

    def answer(i, carry):
        tg = lax.rem(g + i // owners, groups)
        td = lax.rem(d + i % owners, owners)
        pltpu.make_async_remote_copy(
            src_ref=ans.at[:, tg * owners + td, :],
            dst_ref=back.at[:, home, :],
            send_sem=sems.at[2],
            recv_sem=sems.at[3],
            device_id=(tg, td),
            device_id_type=MESH,
        ).start()
        return carry

    lax.fori_loop(1, n, answer, 0)
    own.wait()
    most = back.at[:, pl.ds(0, n - 1), :]
    pltpu.make_async_copy(most, most, sems.at[3]).wait()
    pltpu.make_async_copy(most, most, sems.at[2]).wait()


def finish_kernel(keep, owners, bounds, pos, back, out, slots):
    for r in range(owners):
        rows = slice(r * SUB, (r + 1) * SUB)
        square = jnp.sum(back[ROWS, rows, :], axis=0, keepdims=True)
        extent = jnp.full((1, LANES), bounds[r + 1] - bounds[r], I32).astype(F32)
        rms = jnp.sqrt(square / (extent * 128.0) + 1e-06)
        for i in range(ROWS):
            at = (r * ROWS + i) * SUB
            slots[at : at + SUB, :] = back[i, rows, :] / rms
    slots[...] = swap_blocks(slots[...])

    def take(k, carry):
        out[pl.ds(k, 1), :] = slots[pl.ds(pos[0, k], 1), :]
        return carry

    lax.fori_loop(0, keep, take, 0, unroll=8)


def body(groups, owners, acts, grad_out, error_in, kept, bounds):
    tokens, width = acts.shape
    keep = kept.shape[1]
    pad = -(-keep // LANES) * LANES
    n = groups * owners
    nblocks = width * width // LANES
    base = nblocks // owners
    heights = (base + 2 * (base // 4)) // SUB
    tile = 256
    smem = pl.BlockSpec(memory_space=pltpu.SMEM)
    vmem = pl.BlockSpec(memory_space=pltpu.VMEM)
    new_error, send, pos = pl.pallas_call(
        functools.partial(grads_kernel, keep, owners),
        grid=(width // tile,),
        in_specs=[
            pl.BlockSpec((tokens, tile), lambda i: (0, i)),
            pl.BlockSpec((tokens, width), lambda i: (0, 0)),
            pl.BlockSpec((tile, width), lambda i: (i, 0)),
            pl.BlockSpec((1, keep), lambda i: (0, 0)),
            smem,
            smem,
        ],
        out_specs=[
            pl.BlockSpec((tile, width), lambda i: (i, 0)),
            pl.BlockSpec((ROWS + 1, n, LANES), lambda i: (0, 0, 0)),
            pl.BlockSpec((8, pad), lambda i: (0, 0)),
        ],
        out_shape=[
            jax.ShapeDtypeStruct((width, width), BF16),
            jax.ShapeDtypeStruct((ROWS + 1, n, LANES), F32),
            jax.ShapeDtypeStruct((8, pad), I32),
        ],
        scratch_shapes=[
            pltpu.VMEM((width // LANES, width, LANES), F32),
            pltpu.VMEM((8, pad), I32),
            pltpu.VMEM((pad, LANES), F32),
        ],
        compiler_params=pltpu.CompilerParams(vmem_limit_bytes=56 << 20),
    )(acts, grad_out, error_in, kept, kept, bounds)
    back = pl.pallas_call(
        functools.partial(sums_kernel, groups, owners),
        in_specs=[smem, vmem],
        out_specs=vmem,
        out_shape=jax.ShapeDtypeStruct((ROWS + 1, n, LANES), F32),
        scratch_shapes=[
            pltpu.VMEM((ROWS + 1, n, LANES), F32),
            pltpu.VMEM((ROWS, heights, SUB * n), BF16),
            pltpu.VMEM((ROWS + 1, n, LANES), F32),
            pltpu.VMEM((2, LANES, n), I32),
            pltpu.VMEM((heights, 2 * LANES), F32),
            pltpu.SemaphoreType.DMA((5,)),
            pltpu.SemaphoreType.REGULAR,
        ],
        compiler_params=pltpu.CompilerParams(
            collective_id=0, has_side_effects=True, vmem_limit_bytes=40 << 20
        ),
    )(bounds, send)
    result = pl.pallas_call(
        functools.partial(finish_kernel, keep, owners),
        in_specs=[smem, smem, vmem],
        out_specs=vmem,
        out_shape=jax.ShapeDtypeStruct((keep, LANES), F32),
        scratch_shapes=[pltpu.VMEM((owners * CAP, LANES), F32)],
        compiler_params=pltpu.CompilerParams(vmem_limit_bytes=40 << 20),
    )(bounds, pos, back)
    return new_error, result[None]


def solution(mesh):
    spec = P(("group", "dp"), None)
    return jax.shard_map(
        functools.partial(body, mesh.shape["group"], mesh.shape["dp"]),
        mesh=mesh,
        in_specs=(spec, spec, spec, spec, P()),
        out_specs=(spec, P(("group", "dp"), None, None)),
        check_vma=False,
    )
```

```python
import functools

import jax
import jax.numpy as jnp
from jax import lax
from jax.experimental import pallas as pl
from jax.experimental.pallas import tpu as pltpu
from jax.sharding import PartitionSpec as P

MESH = pl.DeviceIdType.MESH
CAP = 80
SUB = 8
ROWS = CAP // SUB
LANES = 128
WIDE = LANES // SUB
F32, BF16, I32 = jnp.float32, jnp.bfloat16, jnp.int32


def iota(shape, dim):
    return lax.broadcasted_iota(I32, shape, dim)


def onehot(mask):
    return jnp.where(mask, 1.0, 0.0).astype(BF16)


def dot(a, b, ca, cb):
    return lax.dot_general(a, b, (((ca,), (cb,)), ((), ())), preferred_element_type=F32)


def split(x):
    hi = x.astype(BF16)
    return hi, (x - hi.astype(F32)).astype(BF16)


def swap_blocks(x):
    n = x.shape[0]
    row = iota(x.shape, 0) & 7
    blk = iota(x.shape, 1) // WIDE
    for k in (1, 2, 4):
        low_row = (row & k) == 0
        low_blk = (blk & k) == 0
        up = pltpu.roll(pltpu.roll(x, n - k, 0), k * WIDE, 1)
        down = pltpu.roll(pltpu.roll(x, k, 0), LANES - k * WIDE, 1)
        x = jnp.where(low_row == low_blk, x, jnp.where(low_row, up, down))
    return x


def sums_kernel(
    keep, groups, owners, kept, bounds, acts_in, grad_in, err_in,
    err_out, back, pos_out,
    acts, grad, err, ids_s, rows_of, sel, packed, send, got, oh, ans, ct, total, sems, bsem,
):
    g = lax.axis_index("group")
    d = lax.axis_index("dp")
    n = groups * owners
    home = d * groups + g
    heights = oh.shape[1]
    width = err.shape[1]
    pad = ids_s.shape[1]
    half = n // 2
    tile = 256
    shift = (width // LANES).bit_length() - 1
    per_row = width // LANES

    loads = [
        pltpu.make_async_copy(a, b, sems.at[8 + i])
        for i, (a, b) in enumerate(((acts_in, acts), (grad_in, grad), (err_in, err)))
    ]
    for load in loads:
        load.start()
    barrier = pltpu.get_barrier_semaphore()
    for i in range(1, groups):
        pl.semaphore_signal(
            barrier, inc=1, device_id=(lax.rem(g + i, groups), d), device_id_type=MESH
        )
    for i in range(1, owners):
        pl.semaphore_signal(
            barrier, inc=1, device_id=(g, lax.rem(d + i, owners)), device_id_type=MESH
        )

    ids_s[...] = jnp.full(ids_s.shape, -1, I32)
    ids_s[0:1, 0:keep] = kept[...]
    ids = ids_s[0:1, :]
    live = ids >= 0
    idf = ids.astype(F32)
    column = jnp.concatenate(
        [
            jnp.broadcast_to(idf[:, b : b + LANES], (LANES, LANES)).T
            for b in range(0, pad, LANES)
        ],
        axis=0,
    ).astype(I32)
    rho = column >> shift
    kappa = column & (per_row - 1)
    for c in range(per_row):
        rows_of[:, c * LANES : (c + 1) * LANES] = onehot(
            iota((pad, LANES), 1) + c * LANES == rho
        )
    region = jnp.zeros(ids.shape, I32)
    for q in range(1, owners):
        region = region + (ids >= bounds[q]).astype(I32)
    of = (iota((owners, pad), 0) == region) & live
    earlier = onehot(iota((pad, pad), 0) < iota((pad, pad), 1))
    before = dot(onehot(of), earlier, 1, 0)
    slot = jnp.sum(jnp.where(of, before, 0.0), axis=0, keepdims=True).astype(I32)
    pos = jnp.where(live, region * CAP + slot, -1)
    pos_out[...] = jnp.broadcast_to(pos, pos_out.shape)
    at = onehot((iota((LANES, pad), 0) == slot) & live)
    high = jnp.where(of, (ids >> 8).astype(F32), 0.0).astype(BF16)
    low = jnp.where(of, (ids & 255).astype(F32), 0.0).astype(BF16)
    number = dot(high, at, 1, 1) * 256.0 + dot(low, at, 1, 1)
    number = jnp.where(dot(onehot(of), at, 1, 1) > 0.5, number, -1048576.0)

    loads[0].wait()
    sel[...] = dot(rows_of[...], acts[...], 1, 1).astype(BF16)
    pl.semaphore_wait(barrier, groups + owners - 2)
    for i in range(1, groups):
        pl.semaphore_signal(
            bsem, inc=1, device_id=(lax.rem(g + i, groups), d), device_id_type=MESH
        )
    loads[1].wait()
    loads[2].wait()
    vals = jnp.zeros((pad, LANES), F32)
    for c in range(0, width, 4 * LANES):
        cols = slice(c, c + 4 * LANES)
        part = dot(sel[...], grad[:, cols], 1, 0) + dot(rows_of[...], err[:, cols], 1, 0)
        for b in range(4):
            vals = jnp.where(
                kappa == c // LANES + b, part[:, b * LANES : (b + 1) * LANES], vals
            )
    place = onehot((iota((owners * CAP, pad), 0) == pos) & live)
    hi, lo = split(vals)
    packed[...] = swap_blocks(dot(place, hi, 1, 0) + dot(place, lo, 1, 0))
    for r in range(owners):
        for i in range(ROWS):
            tile_at = (r * ROWS + i) * SUB
            send[i, r * SUB : (r + 1) * SUB, :] = packed[tile_at : tile_at + SUB]
        send[ROWS, r * SUB : (r + 1) * SUB, :] = jnp.broadcast_to(
            number[r : r + 1, :], (SUB, LANES)
        )
    pl.semaphore_wait(bsem, groups - 1)

    own = pltpu.make_async_copy(send.at[:, home, :], got.at[:, 0, :], sems.at[6])
    own.start()

    def push(part):
        def one(o, carry):
            tg = lax.rem(g + o // owners, groups)
            td = lax.rem(d + o % owners, owners)
            pltpu.make_async_remote_copy(
                src_ref=send.at[:, td * groups + tg, :],
                dst_ref=got.at[:, o, :],
                send_sem=sems.at[0],
                recv_sem=sems.at[1 + part],
                device_id=(tg, td),
                device_id_type=MESH,
            ).start()
            return carry

        return one

    lax.fori_loop(1, half, push(0), 0)
    lax.fori_loop(half, n, push(1), 0)

    def product(t, carry):
        rows = pl.ds(pl.multiple_of(t * tile, tile), tile)
        hit_row = onehot(iota((tile, pad), 0) + t * tile == ids_s[0:1, :] >> shift)
        hit_col = onehot(iota((LANES, pad), 0) == ids_s[0:1, :] & (per_row - 1))
        cleared = dot(hit_row, hit_col, 1, 1)
        for c in range(0, width, 2 * LANES):
            cols = slice(c, c + 2 * LANES)
            full = dot(acts[:, rows], grad[:, cols], 0, 0) + err[rows, cols].astype(F32)
            for b in range(2):
                at_c = c // LANES + b
                err[rows, at_c * LANES : (at_c + 1) * LANES] = jnp.where(
                    cleared[:, at_c : at_c + 1] > 0.5, 0.0, full[:, b * LANES : (b + 1) * LANES]
                ).astype(BF16)
        return carry

    first = width // tile // 2
    lax.fori_loop(0, first, product, 0)
    upper = pl.ds(0, first * tile)
    stores = [pltpu.make_async_copy(err.at[upper], err_out.at[upper], sems.at[7])]
    stores[0].start()

    total[...] = jnp.zeros(total.shape, F32)
    left = iota((SUB, LANES), 1) < half

    def index_rows(h, p, which):
        at_p = pl.multiple_of(p * 2 * SUB, 2 * SUB)
        return jnp.where(
            left, ct[h, which, pl.ds(at_p, SUB), :], ct[h, which, pl.ds(at_p + SUB, SUB), :]
        )

    def add(h):
        def one(p, carry):
            x = jnp.concatenate(
                [
                    got[2 * p, h * half : (h + 1) * half, :],
                    got[2 * p + 1, h * half : (h + 1) * half, :],
                ],
                axis=0,
            ).T
            hi = x.astype(BF16).astype(F32)
            lo = x - hi
            high = index_rows(h, p, 0)
            low = index_rows(h, p, 1)
            step = h * (ROWS // 2) + p
            parts = []
            for j in range(SUB):
                oh[step, :, j * n : (j + 1) * n] = onehot(
                    iota((heights, n), 0) == high[j : j + 1, :]
                )
                mine = [low[j : j + 1, :] == c for c in range(SUB)]
                rows = slice(j * WIDE, (j + 1) * WIDE)
                parts.append(
                    jnp.concatenate(
                        [jnp.where(m, hi[rows], 0.0).astype(BF16) for m in mine]
                        + [jnp.where(m, lo[rows], 0.0).astype(BF16) for m in mine],
                        axis=0,
                    )
                )
            total[...] += dot(oh[step], jnp.concatenate(parts, axis=1), 1, 1)
            return carry

        return one

    own.wait()
    for h in range(2):
        arrived = got.at[:, pl.ds(0, half - 1 + h), :]
        pltpu.make_async_copy(arrived, arrived, sems.at[1 + h]).wait()
        numbers = got[ROWS, h * half : (h + 1) * half, :]
        local = jnp.concatenate([numbers, numbers], axis=0).T.astype(I32) - bounds[d]
        ct[h, 0] = local >> 3
        ct[h, 1] = local & 7
        lax.fori_loop(0, ROWS // 2, add(h), 0)

    whole = total[:, :LANES] + total[:, LANES:]
    ans[ROWS] = jnp.broadcast_to(jnp.sum(whole * whole, keepdims=True), (n, LANES))
    hi, lo = split(whole.T)
    table = jnp.concatenate([hi, lo], axis=0)

    def look(h):
        def one(p, carry):
            both = dot(table, oh[h * (ROWS // 2) + p], 1, 0)
            both = both[:LANES] + both[LANES:]
            low = index_rows(h, p, 1)
            parts = []
            for j in range(SUB):
                picked = jnp.zeros((WIDE, n), F32)
                for c in range(SUB):
                    picked = jnp.where(
                        low[j : j + 1, :] == c,
                        both[c * WIDE : (c + 1) * WIDE, j * n : (j + 1) * n],
                        picked,
                    )
                parts.append(picked)
            rows = jnp.concatenate(parts, axis=0).T
            ans[2 * p, h * half : (h + 1) * half, :] = rows[:half]
            ans[2 * p + 1, h * half : (h + 1) * half, :] = rows[half:]
            return carry

        return one

    def answer(o, carry):
        tg = lax.rem(g + groups - o // owners, groups)
        td = lax.rem(d + owners - o % owners, owners)
        pltpu.make_async_remote_copy(
            src_ref=ans.at[:, o, :],
            dst_ref=back.at[:, home, :],
            send_sem=sems.at[4],
            recv_sem=sems.at[5],
            device_id=(tg, td),
            device_id_type=MESH,
        ).start()
        return carry

    lax.fori_loop(0, ROWS // 2, look(0), 0)
    own = pltpu.make_async_copy(ans.at[:, 0, :], back.at[:, home, :], sems.at[6])
    own.start()
    lax.fori_loop(1, half, answer, 0)
    lax.fori_loop(0, ROWS // 2, look(1), 0)
    lax.fori_loop(half, n, answer, 0)

    lax.fori_loop(first, width // tile, product, 0)
    stores[0].wait()
    lower = pl.ds(first * tile, width - first * tile)
    stores.append(pltpu.make_async_copy(err.at[lower], err_out.at[lower], sems.at[7]))
    stores[1].start()
    own.wait()
    sent = got.at[:, pl.ds(0, n - 1), :]
    pltpu.make_async_copy(sent, sent, sems.at[0]).wait()
    pltpu.make_async_copy(sent, sent, sems.at[4]).wait()
    came = back.at[:, pl.ds(0, n - 1), :]
    pltpu.make_async_copy(came, came, sems.at[5]).wait()
    stores[1].wait()


def finish_kernel(keep, owners, bounds, pos, back, err_in, out, err_out, slots, held, sems):
    parts = sems.shape[1]
    rows = err_in.shape[0] // parts
    cuts = [pl.ds(i * rows, rows) for i in range(parts)]
    loads = [
        pltpu.make_async_copy(err_in.at[cut], held.at[cut], sems.at[0, i])
        for i, cut in enumerate(cuts)
    ]
    stores = [
        pltpu.make_async_copy(held.at[cut], err_out.at[cut], sems.at[1, i])
        for i, cut in enumerate(cuts)
    ]
    for load in loads:
        load.start()
    for r in range(owners):
        if r % 2 == 0:
            loads[r // 2].wait()
            stores[r // 2].start()
        rows = slice(r * SUB, (r + 1) * SUB)
        square = jnp.sum(back[ROWS, rows, :], axis=0, keepdims=True)
        extent = jnp.full((1, LANES), bounds[r + 1] - bounds[r], I32).astype(F32)
        rms = jnp.sqrt(square / (extent * 128.0) + 1e-06)
        for i in range(ROWS):
            at = (r * ROWS + i) * SUB
            slots[at : at + SUB, :] = back[i, rows, :] / rms
    slots[...] = swap_blocks(slots[...])

    def take(k, carry):
        out[pl.ds(k, 1), :] = slots[pl.ds(pos[0, k], 1), :]
        return carry

    lax.fori_loop(0, keep, take, 0, unroll=8)
    for store in stores:
        store.wait()


def body(groups, owners, acts, grad_out, error_in, kept, bounds):
    tokens, width = acts.shape
    keep = kept.shape[1]
    pad = -(-keep // LANES) * LANES
    n = groups * owners
    nblocks = width * width // LANES
    base = nblocks // owners
    heights = (base + 2 * (base // 4)) // SUB
    smem = pl.BlockSpec(memory_space=pltpu.SMEM)
    vmem = pl.BlockSpec(memory_space=pltpu.VMEM)
    hbm = pl.BlockSpec(memory_space=pl.ANY)
    new_error, back, pos = pl.pallas_call(
        functools.partial(sums_kernel, keep, groups, owners),
        in_specs=[vmem, smem, hbm, hbm, hbm],
        out_specs=[hbm, vmem, vmem],
        out_shape=[
            jax.ShapeDtypeStruct((width, width), BF16),
            jax.ShapeDtypeStruct((ROWS + 1, n, LANES), F32),
            jax.ShapeDtypeStruct((8, pad), I32),
        ],
        scratch_shapes=[
            pltpu.VMEM((tokens, width), BF16),
            pltpu.VMEM((tokens, width), BF16),
            pltpu.VMEM((width, width), BF16),
            pltpu.VMEM((8, pad), I32),
            pltpu.VMEM((pad, width), BF16),
            pltpu.VMEM((pad, tokens), BF16),
            pltpu.VMEM((owners * CAP, LANES), F32),
            pltpu.VMEM((ROWS + 1, n, LANES), F32),
            pltpu.VMEM((ROWS + 1, n, LANES), F32),
            pltpu.VMEM((ROWS, heights, SUB * n), BF16),
            pltpu.VMEM((ROWS + 1, n, LANES), F32),
            pltpu.VMEM((2, 2, LANES, n), I32),
            pltpu.VMEM((heights, 2 * LANES), F32),
            pltpu.SemaphoreType.DMA((11,)),
            pltpu.SemaphoreType.REGULAR,
        ],
        compiler_params=pltpu.CompilerParams(
            collective_id=0, has_side_effects=True, vmem_limit_bytes=60 << 20
        ),
    )(kept, bounds, acts, grad_out, error_in)
    result, new_error = pl.pallas_call(
        functools.partial(finish_kernel, keep, owners),
        in_specs=[smem, smem, vmem, hbm],
        out_specs=[vmem, hbm],
        out_shape=[
            jax.ShapeDtypeStruct((keep, LANES), F32),
            jax.ShapeDtypeStruct((width, width), BF16),
        ],
        scratch_shapes=[
            pltpu.VMEM((owners * CAP, LANES), F32),
            pltpu.VMEM((width, width), BF16),
            pltpu.SemaphoreType.DMA((2, owners // 2)),
        ],
        compiler_params=pltpu.CompilerParams(vmem_limit_bytes=60 << 20),
    )(bounds, pos, back, new_error)
    return new_error, result[None]


def solution(mesh):
    spec = P(("group", "dp"), None)
    return jax.shard_map(
        functools.partial(body, mesh.shape["group"], mesh.shape["dp"]),
        mesh=mesh,
        in_specs=(spec, spec, spec, spec, P()),
        out_specs=(spec, P(("group", "dp"), None, None)),
        check_vma=False,
    )
```

```python
import functools

import jax
import jax.numpy as jnp
from jax import lax
from jax.experimental import pallas as pl
from jax.experimental.pallas import tpu as pltpu
from jax.sharding import PartitionSpec as P

MESH = pl.DeviceIdType.MESH
CAP = 97
SUB = 16
ROWS = 6
LANES = 128
WIDE = LANES // SUB
LAST = (ROWS + 1) * SUB
F32, BF16, I32 = jnp.float32, jnp.bfloat16, jnp.int32


def iota(shape, dim):
    return lax.broadcasted_iota(I32, shape, dim)


def onehot(mask):
    return jnp.where(mask, 1.0, 0.0).astype(BF16)


def dot(a, b, ca, cb):
    return lax.dot_general(a, b, (((ca,), (cb,)), ((), ())), preferred_element_type=F32)


def split(x):
    hi = x.astype(BF16)
    return hi, (x - hi.astype(F32)).astype(BF16)


def swap_blocks(x):
    n = x.shape[0]
    row = iota(x.shape, 0) & (SUB - 1)
    blk = iota(x.shape, 1) // WIDE
    for k in (1, 2, 4, 8):
        low_row = (row & k) == 0
        low_blk = (blk & k) == 0
        up = pltpu.roll(pltpu.roll(x, n - k, 0), k * WIDE, 1)
        down = pltpu.roll(pltpu.roll(x, k, 0), LANES - k * WIDE, 1)
        x = jnp.where(low_row == low_blk, x, jnp.where(low_row, up, down))
    return x


def sums_kernel(
    keep, groups, owners, kept, bounds, acts_in, grad_in, err_in,
    err_out, back, pos_out,
    acts, grad, err, ids_s, rows_of, sel, kept_rows, packed, send, got, oh, oh_last, put, ans, ct,
    total, sems, bsem,
):
    g = lax.axis_index("group")
    d = lax.axis_index("dp")
    n = groups * owners
    me = g * owners + d
    heights = oh.shape[1]
    width = err.shape[1]
    pad = ids_s.shape[1]
    half = n // 2
    tile = 256
    shift = (width // LANES).bit_length() - 1
    per_row = width // LANES

    load_acts = pltpu.make_async_copy(acts_in, acts, sems.at[8])
    load_grad = pltpu.make_async_copy(grad_in, grad, sems.at[9])
    quarter = width // 4
    cuts = [pl.ds(i * quarter, quarter) for i in range(4)]
    load_err = [
        pltpu.make_async_copy(err_in.at[cut], err.at[cut], sems.at[10 + i])
        for i, cut in enumerate(cuts)
    ]
    load_acts.start()
    barrier = pltpu.get_barrier_semaphore()
    for i in range(1, groups):
        pl.semaphore_signal(
            barrier, inc=1, device_id=(lax.rem(g + i, groups), d), device_id_type=MESH
        )
    for i in range(1, owners):
        pl.semaphore_signal(
            barrier, inc=1, device_id=(g, lax.rem(d + i, owners)), device_id_type=MESH
        )

    ids_s[...] = jnp.full(ids_s.shape, -1, I32)
    ids_s[0:1, 0:keep] = kept[...]
    ids = ids_s[0:1, :]
    live = ids >= 0
    idf = ids.astype(F32)
    column = jnp.concatenate(
        [
            jnp.broadcast_to(idf[:, b : b + LANES], (LANES, LANES)).T
            for b in range(0, pad, LANES)
        ],
        axis=0,
    ).astype(I32)
    rho = column >> shift
    kappa = column & (per_row - 1)
    for c in range(per_row):
        rows_of[:, c * LANES : (c + 1) * LANES] = onehot(
            iota((pad, LANES), 1) + c * LANES == rho
        )
    load_grad.start()
    region = jnp.zeros(ids.shape, I32)
    for q in range(1, owners):
        region = region + (ids >= bounds[q]).astype(I32)
    of = (iota((groups, pad), 0) == region >> 1) & live
    earlier = onehot(iota((pad, pad), 0) < iota((pad, pad), 1))
    before = dot(onehot(of), earlier, 1, 0)
    slot = jnp.sum(jnp.where(of, before, 0.0), axis=0, keepdims=True).astype(I32)
    pos = (region >> 1) * LAST + slot + jnp.where(slot == CAP - 1, SUB - 1, 0)
    pos = jnp.where(live, pos, -1)
    pos_out[...] = jnp.broadcast_to(pos * owners + region, pos_out.shape)
    at = onehot((iota((LANES, pad), 0) == slot) & live)
    high = jnp.where(of, (ids >> 8).astype(F32), 0.0).astype(BF16)
    low = jnp.where(of, (ids & 255).astype(F32), 0.0).astype(BF16)
    number = dot(high, at, 1, 1) * 256.0 + dot(low, at, 1, 1)
    number = jnp.where(dot(onehot(of), at, 1, 1) > 0.5, number, -1048576.0)

    load_acts.wait()
    for load in load_err:
        load.start()
    sel[...] = dot(rows_of[...], acts[...], 1, 1).astype(BF16)
    pl.semaphore_wait(barrier, groups + owners - 2)
    for i in range(1, groups):
        pl.semaphore_signal(
            bsem, inc=1, device_id=(lax.rem(g + i, groups), d), device_id_type=MESH
        )
    load_grad.wait()
    kept_rows[...] = dot(sel[...], grad[...], 1, 0)
    for load, cut in zip(load_err[:-1], cuts):
        load.wait()
        kept_rows[...] += dot(rows_of[:, cut], err[cut, :], 1, 0)
    load_err[-1].wait()
    vals = jnp.zeros((pad, LANES), F32)
    for c in range(0, width, 4 * LANES):
        cols = slice(c, c + 4 * LANES)
        part = kept_rows[:, cols] + dot(rows_of[:, cuts[-1]], err[cuts[-1], cols], 1, 0)
        for b in range(4):
            vals = jnp.where(
                kappa == c // LANES + b, part[:, b * LANES : (b + 1) * LANES], vals
            )
    place = onehot((iota((groups * LAST, pad), 0) == pos) & live)
    hi, lo = split(vals)
    packed[...] = swap_blocks(dot(place, hi, 1, 0) + dot(place, lo, 1, 0))
    for q in range(groups):
        rows = slice(q * SUB, (q + 1) * SUB)
        for i in range(ROWS + 1):
            at_q = (q * (ROWS + 1) + i) * SUB
            block = packed[at_q : at_q + SUB]
            if i == ROWS:
                block = jnp.where(
                    iota((SUB, LANES), 1) < LANES - SUB,
                    jnp.broadcast_to(number[q : q + 1, :], (SUB, LANES)),
                    block,
                )
            send[i, rows, :] = block
    pl.semaphore_wait(bsem, groups - 1)

    own = pltpu.make_async_copy(send.at[:, me, :], got.at[:, 0, :], sems.at[6])
    own.start()

    def push(part):
        def one(o, carry):
            tg = lax.rem(g + o // owners, groups)
            td = lax.rem(d + o % owners, owners)
            pltpu.make_async_remote_copy(
                src_ref=send.at[:, tg * owners + td, :],
                dst_ref=got.at[:, o, :],
                send_sem=sems.at[0],
                recv_sem=sems.at[1 + part],
                device_id=(tg, td),
                device_id_type=MESH,
            ).start()
            return carry

        return one

    lax.fori_loop(1, half, push(0), 0)
    lax.fori_loop(half, n, push(1), 0)

    def product(t, carry):
        rows = pl.ds(pl.multiple_of(t * tile, tile), tile)
        hit_row = onehot(iota((tile, pad), 0) + t * tile == ids_s[0:1, :] >> shift)
        hit_col = onehot(iota((LANES, pad), 0) == ids_s[0:1, :] & (per_row - 1))
        cleared = dot(hit_row, hit_col, 1, 1)
        for c in range(0, width, 2 * LANES):
            cols = slice(c, c + 2 * LANES)
            full = dot(acts[:, rows], grad[:, cols], 0, 0) + err[rows, cols].astype(F32)
            for b in range(2):
                at_c = c // LANES + b
                err[rows, at_c * LANES : (at_c + 1) * LANES] = jnp.where(
                    cleared[:, at_c : at_c + 1] > 0.5, 0.0, full[:, b * LANES : (b + 1) * LANES]
                ).astype(BF16)
        return carry

    first = width // tile // 2
    lax.fori_loop(0, first, product, 0)
    upper = pl.ds(0, first * tile)
    stores = [pltpu.make_async_copy(err.at[upper], err_out.at[upper], sems.at[7])]
    stores[0].start()

    total[...] = jnp.zeros(total.shape, F32)
    left = iota((SUB, LANES), 1) < half
    def index_rows(h, p, which):
        at_p = pl.multiple_of(p * 2 * SUB, 2 * SUB)
        return jnp.where(
            left, ct[h, which, pl.ds(at_p, SUB), :], ct[h, which, pl.ds(at_p + SUB, SUB), :]
        )

    def height_of(row):
        return onehot(iota((heights, n), 0) == row)

    def put_of(row, x):
        hi = x.astype(BF16).astype(F32)
        mine = [row == c for c in range(SUB)]
        return [
            jnp.concatenate([jnp.where(m, part, 0.0) for m in mine], axis=0).astype(BF16)
            for part in (hi, x - hi)
        ]

    def add(h):
        def one(p, carry):
            x = jnp.concatenate(
                [
                    got[2 * p, h * half : (h + 1) * half, :],
                    got[2 * p + 1, h * half : (h + 1) * half, :],
                ],
                axis=0,
            ).T
            high = index_rows(h, p, 0)
            low = index_rows(h, p, 1)
            step = h * (ROWS // 2) + p
            for j in range(SUB):
                lanes = slice(j * n, (j + 1) * n)
                oh[step, :, lanes] = height_of(high[j : j + 1, :])
                hi, lo = put_of(low[j : j + 1, :], x[j * WIDE : (j + 1) * WIDE])
                put[:LANES, lanes] = hi
                put[LANES:, lanes] = lo
            total[...] += dot(oh[step], put[...], 1, 1)
            return carry

        return one

    own.wait()
    for h in range(2):
        arrived = got.at[:, pl.ds(0, half - 1 + h), :]
        pltpu.make_async_copy(arrived, arrived, sems.at[1 + h]).wait()
        numbers = got[ROWS, h * half : (h + 1) * half, :]
        local = jnp.concatenate([numbers, numbers], axis=0).T.astype(I32) - bounds[2 * g]
        ct[h, 0] = local >> 4
        ct[h, 1] = local & (SUB - 1)
        lax.fori_loop(0, ROWS // 2, add(h), 0)

    first_half = iota((1, n), 1) < half
    high, low = (
        jnp.where(first_half, ct[0, k, CAP - 1 : CAP, :], ct[1, k, CAP - 1 : CAP, :])
        for k in range(2)
    )
    oh_last[...] = height_of(high)
    parts = put_of(low, got[ROWS].T[LANES - WIDE :])
    total[...] += dot(oh_last[...], jnp.concatenate(parts, axis=0), 1, 1)

    whole = total[:, :LANES] + total[:, LANES:]
    square = whole * whole
    at_block = iota((heights, LANES), 0) * SUB + iota((heights, LANES), 1) // WIDE
    in_first = at_block < bounds[2 * g + 1] - bounds[2 * g]
    squares = [
        jnp.sum(jnp.where(in_first, square, 0.0), keepdims=True),
        jnp.sum(jnp.where(in_first, 0.0, square), keepdims=True),
    ]
    hi, lo = split(whole.T)
    table = jnp.concatenate([hi, lo], axis=0)

    def pick(both, row):
        picked = jnp.zeros((WIDE, n), F32)
        for c in range(SUB):
            picked = jnp.where(row == c, both[c * WIDE : (c + 1) * WIDE], picked)
        return picked

    both = dot(table, oh_last[...], 1, 0)
    last = pick(both[:LANES] + both[LANES:], low)
    last = jnp.concatenate([jnp.zeros((LANES - WIDE, n), F32), last], axis=0).T
    lane = iota((n, LANES), 1)
    ans[ROWS] = jnp.where(
        lane < LANES - SUB, jnp.where(lane < LANES // 2, squares[0], squares[1]), last
    )

    def look(h):
        def one(p, carry):
            both = dot(table, oh[h * (ROWS // 2) + p], 1, 0)
            both = both[:LANES] + both[LANES:]
            low = index_rows(h, p, 1)
            rows = jnp.concatenate(
                [pick(both[:, j * n : (j + 1) * n], low[j : j + 1, :]) for j in range(SUB)], axis=0
            ).T
            ans[2 * p, h * half : (h + 1) * half, :] = rows[:half]
            ans[2 * p + 1, h * half : (h + 1) * half, :] = rows[half:]
            return carry

        return one

    def answer(o, carry):
        tg = lax.rem(g + groups - o // owners, groups)
        td = lax.rem(d + owners - o % owners, owners)
        pltpu.make_async_remote_copy(
            src_ref=ans.at[:, o, :],
            dst_ref=back.at[:, me, :],
            send_sem=sems.at[4],
            recv_sem=sems.at[5],
            device_id=(tg, td),
            device_id_type=MESH,
        ).start()
        return carry

    lax.fori_loop(0, ROWS // 2, look(0), 0)
    own = pltpu.make_async_copy(ans.at[:, 0, :], back.at[:, me, :], sems.at[6])
    own.start()
    lax.fori_loop(1, half, answer, 0)
    lax.fori_loop(0, ROWS // 2, look(1), 0)
    lax.fori_loop(half, n, answer, 0)

    lax.fori_loop(first, width // tile, product, 0)
    stores[0].wait()
    lower = pl.ds(first * tile, width - first * tile)
    stores.append(pltpu.make_async_copy(err.at[lower], err_out.at[lower], sems.at[7]))
    stores[1].start()
    own.wait()
    sent = got.at[:, pl.ds(0, n - 1), :]
    pltpu.make_async_copy(sent, sent, sems.at[0]).wait()
    pltpu.make_async_copy(sent, sent, sems.at[4]).wait()
    came = back.at[:, pl.ds(0, n - 1), :]
    pltpu.make_async_copy(came, came, sems.at[5]).wait()
    stores[1].wait()


def finish_kernel(keep, groups, owners, bounds, pos, back, err_in, out, err_out, slots, scale, sem):
    store = pltpu.make_async_copy(err_in, err_out, sem)
    store.start()
    for q in range(groups):
        rows = slice(q * SUB, (q + 1) * SUB)
        square = jnp.sum(back[ROWS, rows, :], axis=0, keepdims=True)
        for k in range(2):
            r = 2 * q + k
            extent = jnp.full((1, LANES), bounds[r + 1] - bounds[r], I32).astype(F32)
            at = k * LANES // 2
            mean = jnp.broadcast_to(square[:, at : at + 1], (1, LANES)) / (extent * 128.0)
            scale[r : r + 1, :] = 1.0 / jnp.sqrt(mean + 1e-06)
        for i in range(ROWS + 1):
            at = (q * (ROWS + 1) + i) * SUB
            slots[at : at + SUB, :] = back[i, rows, :]
    slots[...] = swap_blocks(slots[...])

    def take(k, carry):
        at = pos[0, k]
        out[pl.ds(k, 1), :] = slots[pl.ds(at >> 4, 1), :] * scale[pl.ds(at & (owners - 1), 1), :]
        return carry

    lax.fori_loop(0, keep, take, 0, unroll=8)
    store.wait()


def body(groups, owners, acts, grad_out, error_in, kept, bounds):
    tokens, width = acts.shape
    keep = kept.shape[1]
    pad = -(-keep // LANES) * LANES
    n = groups * owners
    nblocks = width * width // LANES
    base = nblocks // owners
    heights = 2 * (base + 2 * (base // 4)) // SUB
    smem = pl.BlockSpec(memory_space=pltpu.SMEM)
    vmem = pl.BlockSpec(memory_space=pltpu.VMEM)
    hbm = pl.BlockSpec(memory_space=pl.ANY)
    new_error, back, pos = pl.pallas_call(
        functools.partial(sums_kernel, keep, groups, owners),
        in_specs=[vmem, smem, hbm, hbm, hbm],
        out_specs=[hbm, vmem, vmem],
        out_shape=[
            pltpu.VMEM((width, width), BF16),
            pltpu.VMEM((ROWS + 1, n, LANES), F32),
            pltpu.VMEM((8, pad), I32),
        ],
        scratch_shapes=[
            pltpu.VMEM((tokens, width), BF16),
            pltpu.VMEM((tokens, width), BF16),
            pltpu.VMEM((width, width), BF16),
            pltpu.VMEM((8, pad), I32),
            pltpu.VMEM((pad, width), BF16),
            pltpu.VMEM((pad, tokens), BF16),
            pltpu.VMEM((pad, width), F32),
            pltpu.VMEM((groups * LAST, LANES), F32),
            pltpu.VMEM((ROWS + 1, n, LANES), F32),
            pltpu.VMEM((ROWS + 1, n, LANES), F32),
            pltpu.VMEM((ROWS, heights, SUB * n), BF16),
            pltpu.VMEM((heights, n), BF16),
            pltpu.VMEM((2 * LANES, SUB * n), BF16),
            pltpu.VMEM((ROWS + 1, n, LANES), F32),
            pltpu.VMEM((2, 2, LANES, n), I32),
            pltpu.VMEM((heights, 2 * LANES), F32),
            pltpu.SemaphoreType.DMA((14,)),
            pltpu.SemaphoreType.REGULAR,
        ],
        compiler_params=pltpu.CompilerParams(
            collective_id=0, has_side_effects=True, vmem_limit_bytes=48 << 20
        ),
    )(*(pltpu.with_memory_space_constraint(x, pltpu.HBM) for x in (kept, bounds, acts, grad_out, error_in)))
    result, new_error = pl.pallas_call(
        functools.partial(finish_kernel, keep, groups, owners),
        in_specs=[smem, smem, vmem, hbm],
        out_specs=[vmem, hbm],
        out_shape=[
            jax.ShapeDtypeStruct((keep, LANES), F32),
            jax.ShapeDtypeStruct((width, width), BF16),
        ],
        scratch_shapes=[
            pltpu.VMEM((groups * LAST, LANES), F32),
            pltpu.VMEM((owners, LANES), F32),
            pltpu.SemaphoreType.DMA,
        ],
        compiler_params=pltpu.CompilerParams(vmem_limit_bytes=12 << 20),
    )(bounds, pos, back, new_error)
    return new_error, result[None]


def solution(mesh):
    spec = P(("group", "dp"), None)
    return jax.shard_map(
        functools.partial(body, mesh.shape["group"], mesh.shape["dp"]),
        mesh=mesh,
        in_specs=(spec, spec, spec, spec, P()),
        out_specs=(spec, P(("group", "dp"), None, None)),
        check_vma=False,
    )
```

```python
import functools

import jax
import jax.numpy as jnp
from jax import lax
from jax.experimental import pallas as pl
from jax.experimental.pallas import tpu as pltpu
from jax.sharding import PartitionSpec as P

MESH = pl.DeviceIdType.MESH
CAP = 97
SUB = 16
ROWS = 6
LANES = 128
WIDE = LANES // SUB
LAST = (ROWS + 1) * SUB
F32, BF16, I32 = jnp.float32, jnp.bfloat16, jnp.int32


def iota(shape, dim):
    return lax.broadcasted_iota(I32, shape, dim)


def onehot(mask):
    return jnp.where(mask, 1.0, 0.0).astype(BF16)


def dot(a, b, ca, cb):
    return lax.dot_general(a, b, (((ca,), (cb,)), ((), ())), preferred_element_type=F32)


def split(x):
    hi = x.astype(BF16)
    return hi, (x - hi.astype(F32)).astype(BF16)


def swap_blocks(x):
    n = x.shape[0]
    row = iota(x.shape, 0) & (SUB - 1)
    blk = iota(x.shape, 1) // WIDE
    for k in (1, 2, 4, 8):
        low_row = (row & k) == 0
        low_blk = (blk & k) == 0
        up = pltpu.roll(pltpu.roll(x, n - k, 0), k * WIDE, 1)
        down = pltpu.roll(pltpu.roll(x, k, 0), LANES - k * WIDE, 1)
        x = jnp.where(low_row == low_blk, x, jnp.where(low_row, up, down))
    return x


def sums_kernel(
    keep, groups, owners, kept, bounds, acts_in, grad_in, err_in,
    err_out, back, pos_out,
    acts, grad, err, ids_s, rows_of, sel, kept_rows, packed, send, got, oh, oh_last, put, ans, ct,
    total, sems, bsem,
):
    g = lax.axis_index("group")
    d = lax.axis_index("dp")
    n = groups * owners
    me = g * owners + d
    heights = oh.shape[1]
    width = err.shape[1]
    pad = ids_s.shape[1]
    half = n // 2
    tile = 512
    shift = (width // LANES).bit_length() - 1
    per_row = width // LANES

    load_acts = pltpu.make_async_copy(acts_in, acts, sems.at[8])
    load_grad = pltpu.make_async_copy(grad_in, grad, sems.at[9])
    quarter = width // 4
    cuts = [pl.ds(i * quarter, quarter) for i in range(4)]
    load_err = [
        pltpu.make_async_copy(err_in.at[cut], err.at[cut], sems.at[10 + i])
        for i, cut in enumerate(cuts)
    ]
    load_acts.start()
    barrier = pltpu.get_barrier_semaphore()
    for i in range(1, groups):
        pl.semaphore_signal(
            barrier, inc=1, device_id=(lax.rem(g + i, groups), d), device_id_type=MESH
        )
    for i in range(1, owners):
        pl.semaphore_signal(
            barrier, inc=1, device_id=(g, lax.rem(d + i, owners)), device_id_type=MESH
        )

    ids_s[...] = jnp.full(ids_s.shape, -1, I32)
    ids_s[0:1, 0:keep] = kept[...]
    ids = ids_s[0:1, :]
    live = ids >= 0
    idf = ids.astype(F32)
    column = jnp.concatenate(
        [
            jnp.broadcast_to(idf[:, b : b + LANES], (LANES, LANES)).T
            for b in range(0, pad, LANES)
        ],
        axis=0,
    ).astype(I32)
    rho = column >> shift
    kappa = column & (per_row - 1)
    for c in range(per_row):
        rows_of[:, c * LANES : (c + 1) * LANES] = onehot(
            iota((pad, LANES), 1) + c * LANES == rho
        )
    load_grad.start()
    region = jnp.zeros(ids.shape, I32)
    for q in range(1, owners):
        region = region + (ids >= bounds[q]).astype(I32)
    of = (iota((groups, pad), 0) == region >> 1) & live
    earlier = onehot(iota((pad, pad), 0) < iota((pad, pad), 1))
    before = dot(onehot(of), earlier, 1, 0)
    slot = jnp.sum(jnp.where(of, before, 0.0), axis=0, keepdims=True).astype(I32)
    pos = (region >> 1) * LAST + slot + jnp.where(slot == CAP - 1, SUB - 1, 0)
    pos = jnp.where(live, pos, -1)
    pos_out[...] = jnp.broadcast_to(pos * owners + region, pos_out.shape)
    at = onehot((iota((LANES, pad), 0) == slot) & live)
    high = jnp.where(of, (ids >> 8).astype(F32), 0.0).astype(BF16)
    low = jnp.where(of, (ids & 255).astype(F32), 0.0).astype(BF16)
    number = dot(high, at, 1, 1) * 256.0 + dot(low, at, 1, 1)
    number = jnp.where(dot(onehot(of), at, 1, 1) > 0.5, number, -1048576.0)

    load_acts.wait()
    for load in load_err:
        load.start()
    sel[...] = dot(rows_of[...], acts[...], 1, 1).astype(BF16)
    pl.semaphore_wait(barrier, groups + owners - 2)
    for i in range(1, groups):
        pl.semaphore_signal(
            bsem, inc=1, device_id=(lax.rem(g + i, groups), d), device_id_type=MESH
        )
    load_grad.wait()
    kept_rows[...] = dot(sel[...], grad[...], 1, 0)
    for load, cut in zip(load_err[:-1], cuts):
        load.wait()
        kept_rows[...] += dot(rows_of[:, cut], err[cut, :], 1, 0)
    load_err[-1].wait()
    vals = jnp.zeros((pad, LANES), F32)
    for c in range(0, width, 4 * LANES):
        cols = slice(c, c + 4 * LANES)
        part = kept_rows[:, cols] + dot(rows_of[:, cuts[-1]], err[cuts[-1], cols], 1, 0)
        for b in range(4):
            vals = jnp.where(
                kappa == c // LANES + b, part[:, b * LANES : (b + 1) * LANES], vals
            )
    place = onehot((iota((groups * LAST, pad), 0) == pos) & live)
    hi, lo = split(vals)
    packed[...] = swap_blocks(dot(place, hi, 1, 0) + dot(place, lo, 1, 0))
    for q in range(groups):
        rows = slice(q * SUB, (q + 1) * SUB)
        for i in range(ROWS + 1):
            at_q = (q * (ROWS + 1) + i) * SUB
            block = packed[at_q : at_q + SUB]
            if i == ROWS:
                block = jnp.where(
                    iota((SUB, LANES), 1) < LANES - SUB,
                    jnp.broadcast_to(number[q : q + 1, :], (SUB, LANES)),
                    block,
                )
            send[i, rows, :] = block
    pl.semaphore_wait(bsem, groups - 1)

    own = pltpu.make_async_copy(send.at[:, me, :], got.at[:, 0, :], sems.at[6])
    own.start()

    def push(o):
        tg = lax.rem(g + o // owners, groups)
        td = lax.rem(d + o % owners, owners)
        pltpu.make_async_remote_copy(
            src_ref=send.at[:, tg * owners + td, :],
            dst_ref=got.at[:, o, :],
            send_sem=sems.at[0],
            recv_sem=sems.at[1 + o // half],
            device_id=(tg, td),
            device_id_type=MESH,
        ).start()

    def product(t, carry):
        rows = pl.ds(pl.multiple_of(t * tile, tile), tile)
        hit_row = onehot(iota((tile, pad), 0) + t * tile == ids_s[0:1, :] >> shift)
        hit_col = onehot(iota((LANES, pad), 0) == ids_s[0:1, :] & (per_row - 1))
        cleared = dot(hit_row, hit_col, 1, 1)
        for c in range(0, width, 2 * LANES):
            cols = slice(c, c + 2 * LANES)
            full = dot(acts[:, rows], grad[:, cols], 0, 0) + err[rows, cols].astype(F32)
            for b in range(2):
                at_c = c // LANES + b
                err[rows, at_c * LANES : (at_c + 1) * LANES] = jnp.where(
                    cleared[:, at_c : at_c + 1] > 0.5, 0.0, full[:, b * LANES : (b + 1) * LANES]
                ).astype(BF16)
        return carry

    def each(start):
        def one(o, carry):
            start(o)
            return carry

        return one

    lax.fori_loop(1, n, each(push), 0)
    first = width // tile // 2
    lax.fori_loop(0, first, product, 0)
    upper = pl.ds(0, first * tile)
    stores = [pltpu.make_async_copy(err.at[upper], err_out.at[upper], sems.at[7])]
    stores[0].start()

    total[...] = jnp.zeros(total.shape, F32)
    left = iota((SUB, LANES), 1) < half
    def index_rows(h, p, which):
        at_p = p * 2 * SUB
        return jnp.where(
            left, ct[h, which, at_p : at_p + SUB, :], ct[h, which, at_p + SUB : at_p + 2 * SUB, :]
        )

    def height_of(row):
        return onehot(iota((heights, n), 0) == row)

    def put_of(row, x):
        hi = x.astype(BF16).astype(F32)
        mine = [row == c for c in range(SUB)]
        return [
            jnp.concatenate([jnp.where(m, part, 0.0) for m in mine], axis=0).astype(BF16)
            for part in (hi, x - hi)
        ]

    def add(h):
        for p in range(ROWS // 2):
            x = jnp.concatenate(
                [
                    got[2 * p, h * half : (h + 1) * half, :],
                    got[2 * p + 1, h * half : (h + 1) * half, :],
                ],
                axis=0,
            ).T
            high = index_rows(h, p, 0)
            low = index_rows(h, p, 1)
            step = h * (ROWS // 2) + p
            for j in range(SUB):
                lanes = slice(j * n, (j + 1) * n)
                oh[step, :, lanes] = height_of(high[j : j + 1, :])
                hi, lo = put_of(low[j : j + 1, :], x[j * WIDE : (j + 1) * WIDE])
                put[step % 2, :LANES, lanes] = hi
                put[step % 2, LANES:, lanes] = lo
            total[...] += dot(put[step % 2], oh[step], 1, 1)

    own.wait()
    for h in range(2):
        arrived = got.at[:, pl.ds(0, half - 1 + h), :]
        pltpu.make_async_copy(arrived, arrived, sems.at[1 + h]).wait()
        numbers = got[ROWS, h * half : (h + 1) * half, :]
        local = jnp.concatenate([numbers, numbers], axis=0).T.astype(I32) - bounds[2 * g]
        ct[h, 0] = local >> 4
        ct[h, 1] = local & (SUB - 1)
        add(h)

    first_half = iota((1, n), 1) < half
    high, low = (
        jnp.where(first_half, ct[0, k, CAP - 1 : CAP, :], ct[1, k, CAP - 1 : CAP, :])
        for k in range(2)
    )
    oh_last[...] = height_of(high)
    parts = put_of(low, got[ROWS].T[LANES - WIDE :])
    total[...] += dot(jnp.concatenate(parts, axis=0), oh_last[...], 1, 1)

    whole = total[:LANES] + total[LANES:]
    square = whole * whole
    at_block = iota((LANES, heights), 1) * SUB + iota((LANES, heights), 0) // WIDE
    in_first = at_block < bounds[2 * g + 1] - bounds[2 * g]
    squares = [
        jnp.sum(jnp.where(in_first, square, 0.0), keepdims=True),
        jnp.sum(jnp.where(in_first, 0.0, square), keepdims=True),
    ]
    hi, lo = split(whole)
    table = jnp.concatenate([hi, lo], axis=0)

    def pick(both, row):
        picked = jnp.zeros((WIDE, n), F32)
        for c in range(SUB):
            picked = jnp.where(row == c, both[c * WIDE : (c + 1) * WIDE], picked)
        return picked

    both = dot(table, oh_last[...], 1, 0)
    last = pick(both[:LANES] + both[LANES:], low)
    last = jnp.concatenate([jnp.zeros((LANES - WIDE, n), F32), last], axis=0).T
    lane = iota((n, LANES), 1)
    ans[ROWS] = jnp.where(
        lane < LANES - SUB, jnp.where(lane < LANES // 2, squares[0], squares[1]), last
    )

    def answer(o):
        tg = lax.rem(g + groups - o // owners, groups)
        td = lax.rem(d + owners - o % owners, owners)
        pltpu.make_async_remote_copy(
            src_ref=ans.at[:, o, :],
            dst_ref=back.at[:, me, :],
            send_sem=sems.at[4],
            recv_sem=sems.at[5],
            device_id=(tg, td),
            device_id_type=MESH,
        ).start()

    def look(h):
        quad = SUB // 4
        for p in range(ROWS // 2):
            low = index_rows(h, p, 1)
            parts = []
            for k in range(4):
                cols = slice(k * quad * n, (k + 1) * quad * n)
                both = dot(table, oh[h * (ROWS // 2) + p, :, cols], 1, 0)
                both = both[:LANES] + both[LANES:]
                for j in range(quad):
                    row = low[k * quad + j : k * quad + j + 1, :]
                    parts.append(pick(both[:, j * n : (j + 1) * n], row))
            rows = jnp.concatenate(parts, axis=0).T
            ans[2 * p, h * half : (h + 1) * half, :] = rows[:half]
            ans[2 * p + 1, h * half : (h + 1) * half, :] = rows[half:]

    look(0)
    own = pltpu.make_async_copy(ans.at[:, 0, :], back.at[:, me, :], sems.at[6])
    own.start()
    lax.fori_loop(1, half, each(answer), 0)
    look(1)
    lax.fori_loop(half, n, each(answer), 0)
    lax.fori_loop(first, width // tile, product, 0)
    stores[0].wait()
    lower = pl.ds(first * tile, width - first * tile)
    stores.append(pltpu.make_async_copy(err.at[lower], err_out.at[lower], sems.at[7]))
    stores[1].start()
    own.wait()
    sent = got.at[:, pl.ds(0, n - 1), :]
    pltpu.make_async_copy(sent, sent, sems.at[0]).wait()
    pltpu.make_async_copy(sent, sent, sems.at[4]).wait()
    came = back.at[:, pl.ds(0, n - 1), :]
    pltpu.make_async_copy(came, came, sems.at[5]).wait()
    stores[1].wait()


def finish_kernel(keep, groups, owners, bounds, pos, back, err_in, out, err_out, slots, scale, sem):
    store = pltpu.make_async_copy(err_in, err_out, sem)
    store.start()
    for q in range(groups):
        rows = slice(q * SUB, (q + 1) * SUB)
        square = jnp.sum(back[ROWS, rows, :], axis=0, keepdims=True)
        for k in range(2):
            r = 2 * q + k
            extent = jnp.full((1, LANES), bounds[r + 1] - bounds[r], I32).astype(F32)
            at = k * LANES // 2
            mean = jnp.broadcast_to(square[:, at : at + 1], (1, LANES)) / (extent * 128.0)
            scale[r : r + 1, :] = 1.0 / jnp.sqrt(mean + 1e-06)
        for i in range(ROWS + 1):
            at = (q * (ROWS + 1) + i) * SUB
            slots[at : at + SUB, :] = back[i, rows, :]
    slots[...] = swap_blocks(slots[...])

    def take(k, carry):
        at = pos[0, k]
        out[pl.ds(k, 1), :] = slots[pl.ds(at >> 4, 1), :] * scale[pl.ds(at & (owners - 1), 1), :]
        return carry

    lax.fori_loop(0, keep, take, 0, unroll=8)
    store.wait()


def body(groups, owners, acts, grad_out, error_in, kept, bounds):
    tokens, width = acts.shape
    keep = kept.shape[1]
    pad = -(-keep // LANES) * LANES
    n = groups * owners
    nblocks = width * width // LANES
    base = nblocks // owners
    heights = 2 * (base + 2 * (base // 4)) // SUB
    smem = pl.BlockSpec(memory_space=pltpu.SMEM)
    vmem = pl.BlockSpec(memory_space=pltpu.VMEM)
    hbm = pl.BlockSpec(memory_space=pl.ANY)
    new_error, back, pos = pl.pallas_call(
        functools.partial(sums_kernel, keep, groups, owners),
        in_specs=[vmem, smem, hbm, hbm, hbm],
        out_specs=[hbm, vmem, vmem],
        out_shape=[
            pltpu.VMEM((width, width), BF16),
            pltpu.VMEM((ROWS + 1, n, LANES), F32),
            pltpu.VMEM((8, pad), I32),
        ],
        scratch_shapes=[
            pltpu.VMEM((tokens, width), BF16),
            pltpu.VMEM((tokens, width), BF16),
            pltpu.VMEM((width, width), BF16),
            pltpu.VMEM((8, pad), I32),
            pltpu.VMEM((pad, width), BF16),
            pltpu.VMEM((pad, tokens), BF16),
            pltpu.VMEM((pad, width), F32),
            pltpu.VMEM((groups * LAST, LANES), F32),
            pltpu.VMEM((ROWS + 1, n, LANES), F32),
            pltpu.VMEM((ROWS + 1, n, LANES), F32),
            pltpu.VMEM((ROWS, heights, SUB * n), BF16),
            pltpu.VMEM((heights, n), BF16),
            pltpu.VMEM((2, 2 * LANES, SUB * n), BF16),
            pltpu.VMEM((ROWS + 1, n, LANES), F32),
            pltpu.VMEM((2, 2, LANES, n), I32),
            pltpu.VMEM((2 * LANES, heights), F32),
            pltpu.SemaphoreType.DMA((14,)),
            pltpu.SemaphoreType.REGULAR,
        ],
        compiler_params=pltpu.CompilerParams(
            collective_id=0, has_side_effects=True, vmem_limit_bytes=48 << 20
        ),
    )(*(pltpu.with_memory_space_constraint(x, pltpu.HBM) for x in (kept, bounds, acts, grad_out, error_in)))
    result, new_error = pl.pallas_call(
        functools.partial(finish_kernel, keep, groups, owners),
        in_specs=[smem, smem, vmem, hbm],
        out_specs=[vmem, hbm],
        out_shape=[
            jax.ShapeDtypeStruct((keep, LANES), F32),
            jax.ShapeDtypeStruct((width, width), BF16),
        ],
        scratch_shapes=[
            pltpu.VMEM((groups * LAST, LANES), F32),
            pltpu.VMEM((owners, LANES), F32),
            pltpu.SemaphoreType.DMA,
        ],
        compiler_params=pltpu.CompilerParams(vmem_limit_bytes=12 << 20),
    )(bounds, pos, back, new_error)
    return new_error, result[None]


def solution(mesh):
    spec = P(("group", "dp"), None)
    return jax.shard_map(
        functools.partial(body, mesh.shape["group"], mesh.shape["dp"]),
        mesh=mesh,
        in_specs=(spec, spec, spec, spec, P()),
        out_specs=(spec, P(("group", "dp"), None, None)),
        check_vma=False,
    )
```

```python
import functools

import jax
import jax.numpy as jnp
from jax import lax
from jax.experimental import pallas as pl
from jax.experimental.pallas import tpu as pltpu
from jax.sharding import PartitionSpec as P

MESH = pl.DeviceIdType.MESH
CAP = 97
SUB = 16
ROWS = 6
LANES = 128
WIDE = LANES // SUB
LAST = (ROWS + 1) * SUB
F32, BF16, I32 = jnp.float32, jnp.bfloat16, jnp.int32


def iota(shape, dim):
    return lax.broadcasted_iota(I32, shape, dim)


def onehot(mask):
    return jnp.where(mask, 1.0, 0.0).astype(BF16)


def dot(a, b, ca, cb):
    return lax.dot_general(a, b, (((ca,), (cb,)), ((), ())), preferred_element_type=F32)


def split(x):
    hi = x.astype(BF16)
    return hi, (x - hi.astype(F32)).astype(BF16)


def swap_blocks(x):
    n = x.shape[0]
    row = iota(x.shape, 0) & (SUB - 1)
    blk = iota(x.shape, 1) // WIDE
    for k in (1, 2, 4, 8):
        low_row = (row & k) == 0
        low_blk = (blk & k) == 0
        up = pltpu.roll(pltpu.roll(x, n - k, 0), k * WIDE, 1)
        down = pltpu.roll(pltpu.roll(x, k, 0), LANES - k * WIDE, 1)
        x = jnp.where(low_row == low_blk, x, jnp.where(low_row, up, down))
    return x


def sums_kernel(
    keep, groups, owners, kept, bounds, acts_in, grad_in, err_in,
    err_out, back, pos_out,
    acts, grad, err, ids_s, rows_of, sel, kept_rows, packed, send, got, oh, oh_last, put, ans, ct,
    total, sems, bsem,
):
    g = lax.axis_index("group")
    d = lax.axis_index("dp")
    n = groups * owners
    me = g * owners + d
    heights = oh.shape[1]
    width = err.shape[1]
    pad = ids_s.shape[1]
    half = n // 2
    tile = 512
    shift = (width // LANES).bit_length() - 1
    per_row = width // LANES

    load_acts = pltpu.make_async_copy(acts_in, acts, sems.at[8])
    load_grad = pltpu.make_async_copy(grad_in, grad, sems.at[9])
    quarter = width // 4
    cuts = [pl.ds(i * quarter, quarter) for i in range(4)]
    load_err = [
        pltpu.make_async_copy(err_in.at[cut], err.at[cut], sems.at[10 + i])
        for i, cut in enumerate(cuts)
    ]
    load_acts.start()
    barrier = pltpu.get_barrier_semaphore()
    for i in range(1, groups):
        pl.semaphore_signal(
            barrier, inc=1, device_id=(lax.rem(g + i, groups), d), device_id_type=MESH
        )
    for i in range(1, owners):
        pl.semaphore_signal(
            barrier, inc=1, device_id=(g, lax.rem(d + i, owners)), device_id_type=MESH
        )

    ids_s[...] = jnp.full(ids_s.shape, -1, I32)
    ids_s[0:1, 0:keep] = kept[...]
    ids = ids_s[0:1, :]
    live = ids >= 0
    idf = ids.astype(F32)
    column = jnp.concatenate(
        [
            jnp.broadcast_to(idf[:, b : b + LANES], (LANES, LANES)).T
            for b in range(0, pad, LANES)
        ],
        axis=0,
    ).astype(I32)
    rho = column >> shift
    kappa = column & (per_row - 1)
    for c in range(per_row):
        rows_of[:, c * LANES : (c + 1) * LANES] = onehot(
            iota((pad, LANES), 1) + c * LANES == rho
        )
    load_grad.start()
    region = jnp.zeros(ids.shape, I32)
    for q in range(1, owners):
        region = region + (ids >= bounds[q]).astype(I32)
    of = (iota((groups, pad), 0) == region >> 1) & live
    earlier = onehot(iota((pad, pad), 0) < iota((pad, pad), 1))
    before = dot(onehot(of), earlier, 1, 0)
    slot = jnp.sum(jnp.where(of, before, 0.0), axis=0, keepdims=True).astype(I32)
    pos = (region >> 1) * LAST + slot + jnp.where(slot == CAP - 1, SUB - 1, 0)
    pos = jnp.where(live, pos, -1)
    pos_out[...] = pos * owners + region
    at = onehot((iota((LANES, pad), 0) == slot) & live)
    high = jnp.where(of, (ids >> 8).astype(F32), 0.0).astype(BF16)
    low = jnp.where(of, (ids & 255).astype(F32), 0.0).astype(BF16)
    number = dot(high, at, 1, 1) * 256.0 + dot(low, at, 1, 1)
    number = jnp.where(dot(onehot(of), at, 1, 1) > 0.5, number, -1048576.0)

    load_acts.wait()
    for load in load_err:
        load.start()
    sel[...] = dot(rows_of[...], acts[...], 1, 1).astype(BF16)
    pl.semaphore_wait(barrier, groups + owners - 2)
    for i in range(1, groups):
        pl.semaphore_signal(
            bsem, inc=1, device_id=(lax.rem(g + i, groups), d), device_id_type=MESH
        )
    load_grad.wait()
    kept_rows[...] = dot(sel[...], grad[...], 1, 0)
    for load in load_err:
        load.wait()
    vals = jnp.zeros((pad, LANES), F32)
    for c in range(0, width, 4 * LANES):
        cols = slice(c, c + 4 * LANES)
        part = kept_rows[:, cols] + dot(rows_of[...], err[:, cols], 1, 0)
        for b in range(4):
            vals = jnp.where(
                kappa == c // LANES + b, part[:, b * LANES : (b + 1) * LANES], vals
            )
    place = onehot((iota((groups * LAST, pad), 0) == pos) & live)
    hi, lo = split(vals)
    packed[...] = swap_blocks(dot(place, hi, 1, 0) + dot(place, lo, 1, 0))
    for q in range(groups):
        rows = slice(q * SUB, (q + 1) * SUB)
        for i in range(ROWS + 1):
            at_q = (q * (ROWS + 1) + i) * SUB
            block = packed[at_q : at_q + SUB]
            if i == ROWS:
                block = jnp.where(
                    iota((SUB, LANES), 1) < LANES - SUB,
                    jnp.broadcast_to(number[q : q + 1, :], (SUB, LANES)),
                    block,
                )
            send[i, rows, :] = block
    pl.semaphore_wait(bsem, groups - 1)

    own = pltpu.make_async_copy(send.at[:, me, :], got.at[:, 0, :], sems.at[6])
    own.start()

    def push(o):
        tg = lax.rem(g + o // owners, groups)
        td = lax.rem(d + o % owners, owners)
        pltpu.make_async_remote_copy(
            src_ref=send.at[:, tg * owners + td, :],
            dst_ref=got.at[:, o, :],
            send_sem=sems.at[0],
            recv_sem=sems.at[1 + o // half],
            device_id=(tg, td),
            device_id_type=MESH,
        ).start()

    def product(t, carry):
        rows = pl.ds(pl.multiple_of(t * tile, tile), tile)
        hit_row = onehot(iota((tile, pad), 0) + t * tile == ids_s[0:1, :] >> shift)
        hit_col = onehot(iota((LANES, pad), 0) == ids_s[0:1, :] & (per_row - 1))
        cleared = dot(hit_row, hit_col, 1, 1)
        for c in range(0, width, 2 * LANES):
            cols = slice(c, c + 2 * LANES)
            full = dot(acts[:, rows], grad[:, cols], 0, 0) + err[rows, cols].astype(F32)
            for b in range(2):
                at_c = c // LANES + b
                err[rows, at_c * LANES : (at_c + 1) * LANES] = jnp.where(
                    cleared[:, at_c : at_c + 1] > 0.5, 0.0, full[:, b * LANES : (b + 1) * LANES]
                ).astype(BF16)
        return carry

    def each(start):
        def one(o, carry):
            start(o)
            return carry

        return one

    lax.fori_loop(1, n, each(push), 0)
    first = width // tile // 2
    lax.fori_loop(0, first, product, 0)
    upper = pl.ds(0, first * tile)
    stores = [pltpu.make_async_copy(err.at[upper], err_out.at[upper], sems.at[7])]
    stores[0].start()

    total[...] = jnp.zeros(total.shape, F32)
    left = iota((SUB, LANES), 1) < half
    def index_rows(h, p, which):
        at_p = p * 2 * SUB
        return jnp.where(
            left, ct[h, which, at_p : at_p + SUB, :], ct[h, which, at_p + SUB : at_p + 2 * SUB, :]
        )

    def height_of(row):
        return onehot(iota((heights, n), 0) == row)

    def put_of(row, x):
        hi = x.astype(BF16).astype(F32)
        mine = [row == c for c in range(SUB)]
        return [
            jnp.concatenate([jnp.where(m, part, 0.0) for m in mine], axis=0).astype(BF16)
            for part in (hi, x - hi)
        ]

    def add(h):
        for p in range(ROWS // 2):
            x = jnp.concatenate(
                [
                    got[2 * p, h * half : (h + 1) * half, :],
                    got[2 * p + 1, h * half : (h + 1) * half, :],
                ],
                axis=0,
            ).T
            high = index_rows(h, p, 0)
            low = index_rows(h, p, 1)
            step = h * (ROWS // 2) + p
            for j in range(SUB):
                lanes = slice(j * n, (j + 1) * n)
                oh[step, :, lanes] = height_of(high[j : j + 1, :])
                hi, lo = put_of(low[j : j + 1, :], x[j * WIDE : (j + 1) * WIDE])
                put[step % 2, :LANES, lanes] = hi
                put[step % 2, LANES:, lanes] = lo
            total[...] += dot(put[step % 2], oh[step], 1, 1)

    own.wait()
    for h in range(2):
        arrived = got.at[:, pl.ds(0, half - 1 + h), :]
        pltpu.make_async_copy(arrived, arrived, sems.at[1 + h]).wait()
        numbers = got[ROWS, h * half : (h + 1) * half, :]
        local = jnp.concatenate([numbers, numbers], axis=0).T.astype(I32) - bounds[2 * g]
        ct[h, 0] = local >> 4
        ct[h, 1] = local & (SUB - 1)
        add(h)

    first_half = iota((1, n), 1) < half
    high, low = (
        jnp.where(first_half, ct[0, k, CAP - 1 : CAP, :], ct[1, k, CAP - 1 : CAP, :])
        for k in range(2)
    )
    oh_last[...] = height_of(high)
    parts = put_of(low, got[ROWS].T[LANES - WIDE :])
    total[...] += dot(jnp.concatenate(parts, axis=0), oh_last[...], 1, 1)

    whole = total[:LANES] + total[LANES:]
    square = whole * whole
    at_block = iota((LANES, heights), 1) * SUB + iota((LANES, heights), 0) // WIDE
    in_first = at_block < bounds[2 * g + 1] - bounds[2 * g]
    squares = [
        jnp.sum(jnp.where(in_first, square, 0.0), keepdims=True),
        jnp.sum(jnp.where(in_first, 0.0, square), keepdims=True),
    ]
    hi, lo = split(whole)
    table = jnp.concatenate([hi, lo], axis=0)

    def pick(both, row):
        picked = jnp.zeros((WIDE, n), F32)
        for c in range(SUB):
            picked = jnp.where(row == c, both[c * WIDE : (c + 1) * WIDE], picked)
        return picked

    both = dot(table, oh_last[...], 1, 0)
    last = pick(both[:LANES] + both[LANES:], low)
    last = jnp.concatenate([jnp.zeros((LANES - WIDE, n), F32), last], axis=0).T
    lane = iota((n, LANES), 1)
    ans[ROWS] = jnp.where(
        lane < LANES - SUB, jnp.where(lane < LANES // 2, squares[0], squares[1]), last
    )

    def answer(o):
        tg = lax.rem(g + groups - o // owners, groups)
        td = lax.rem(d + owners - o % owners, owners)
        pltpu.make_async_remote_copy(
            src_ref=ans.at[:, o, :],
            dst_ref=back.at[:, me, :],
            send_sem=sems.at[4],
            recv_sem=sems.at[5],
            device_id=(tg, td),
            device_id_type=MESH,
        ).start()

    def look(h):
        quad = SUB // 4
        for p in range(ROWS // 2):
            low = index_rows(h, p, 1)
            parts = []
            for k in range(4):
                cols = slice(k * quad * n, (k + 1) * quad * n)
                both = dot(table, oh[h * (ROWS // 2) + p, :, cols], 1, 0)
                both = both[:LANES] + both[LANES:]
                for j in range(quad):
                    row = low[k * quad + j : k * quad + j + 1, :]
                    parts.append(pick(both[:, j * n : (j + 1) * n], row))
            rows = jnp.concatenate(parts, axis=0).T
            ans[2 * p, h * half : (h + 1) * half, :] = rows[:half]
            ans[2 * p + 1, h * half : (h + 1) * half, :] = rows[half:]

    look(0)
    own = pltpu.make_async_copy(ans.at[:, 0, :], back.at[:, me, :], sems.at[6])
    own.start()
    lax.fori_loop(1, half, each(answer), 0)
    look(1)
    lax.fori_loop(half, n, each(answer), 0)
    lax.fori_loop(first, width // tile, product, 0)
    stores[0].wait()
    lower = pl.ds(first * tile, width - first * tile)
    stores.append(pltpu.make_async_copy(err.at[lower], err_out.at[lower], sems.at[7]))
    stores[1].start()
    own.wait()
    sent = got.at[:, pl.ds(0, n - 1), :]
    pltpu.make_async_copy(sent, sent, sems.at[0]).wait()
    pltpu.make_async_copy(sent, sent, sems.at[4]).wait()
    came = back.at[:, pl.ds(0, n - 1), :]
    pltpu.make_async_copy(came, came, sems.at[5]).wait()
    stores[1].wait()


def finish_kernel(keep, groups, owners, bounds, pos, back, err_in, out, err_out, slots, scale, sem):
    store = pltpu.make_async_copy(err_in, err_out, sem)
    store.start()
    for q in range(groups):
        rows = slice(q * SUB, (q + 1) * SUB)
        square = jnp.sum(back[ROWS, rows, :], axis=0, keepdims=True)
        for k in range(2):
            r = 2 * q + k
            extent = jnp.full((1, LANES), bounds[r + 1] - bounds[r], I32).astype(F32)
            at = k * LANES // 2
            mean = jnp.broadcast_to(square[:, at : at + 1], (1, LANES)) / (extent * 128.0)
            scale[r : r + 1, :] = 1.0 / jnp.sqrt(mean + 1e-06)
        for i in range(ROWS + 1):
            at = (q * (ROWS + 1) + i) * SUB
            slots[at : at + SUB, :] = back[i, rows, :]
    slots[...] = swap_blocks(slots[...])

    def take(k, carry):
        at = pos[0, k]
        out[pl.ds(k, 1), :] = slots[pl.ds(at >> 4, 1), :] * scale[pl.ds(at & (owners - 1), 1), :]
        return carry

    lax.fori_loop(0, keep, take, 0, unroll=8)
    store.wait()


def body(groups, owners, acts, grad_out, error_in, kept, bounds):
    tokens, width = acts.shape
    keep = kept.shape[1]
    pad = -(-keep // LANES) * LANES
    n = groups * owners
    nblocks = width * width // LANES
    base = nblocks // owners
    heights = 2 * (base + 2 * (base // 4)) // SUB
    smem = pl.BlockSpec(memory_space=pltpu.SMEM)
    vmem = pl.BlockSpec(memory_space=pltpu.VMEM)
    hbm = pl.BlockSpec(memory_space=pl.ANY)
    new_error, back, pos = pl.pallas_call(
        functools.partial(sums_kernel, keep, groups, owners),
        in_specs=[vmem, smem, hbm, hbm, hbm],
        out_specs=[hbm, vmem, vmem],
        out_shape=[
            pltpu.VMEM((width, width), BF16),
            pltpu.VMEM((ROWS + 1, n, LANES), F32),
            pltpu.VMEM((1, pad), I32),
        ],
        scratch_shapes=[
            pltpu.VMEM((tokens, width), BF16),
            pltpu.VMEM((tokens, width), BF16),
            pltpu.VMEM((width, width), BF16),
            pltpu.VMEM((8, pad), I32),
            pltpu.VMEM((pad, width), BF16),
            pltpu.VMEM((pad, tokens), BF16),
            pltpu.VMEM((pad, width), F32),
            pltpu.VMEM((groups * LAST, LANES), F32),
            pltpu.VMEM((ROWS + 1, n, LANES), F32),
            pltpu.VMEM((ROWS + 1, n, LANES), F32),
            pltpu.VMEM((ROWS, heights, SUB * n), BF16),
            pltpu.VMEM((heights, n), BF16),
            pltpu.VMEM((2, 2 * LANES, SUB * n), BF16),
            pltpu.VMEM((ROWS + 1, n, LANES), F32),
            pltpu.VMEM((2, 2, LANES, n), I32),
            pltpu.VMEM((2 * LANES, heights), F32),
            pltpu.SemaphoreType.DMA((14,)),
            pltpu.SemaphoreType.REGULAR,
        ],
        compiler_params=pltpu.CompilerParams(
            collective_id=0, has_side_effects=True, vmem_limit_bytes=48 << 20
        ),
    )(*(pltpu.with_memory_space_constraint(x, pltpu.HBM) for x in (kept, bounds, acts, grad_out, error_in)))
    result, new_error = pl.pallas_call(
        functools.partial(finish_kernel, keep, groups, owners),
        in_specs=[smem, smem, vmem, hbm],
        out_specs=[vmem, hbm],
        out_shape=[
            jax.ShapeDtypeStruct((keep, LANES), F32),
            jax.ShapeDtypeStruct((width, width), BF16),
        ],
        scratch_shapes=[
            pltpu.VMEM((groups * LAST, LANES), F32),
            pltpu.VMEM((owners, LANES), F32),
            pltpu.SemaphoreType.DMA,
        ],
        compiler_params=pltpu.CompilerParams(vmem_limit_bytes=12 << 20),
    )(bounds, pos, back, new_error)
    return new_error, result[None]


def solution(mesh):
    spec = P(("group", "dp"), None)
    return jax.shard_map(
        functools.partial(body, mesh.shape["group"], mesh.shape["dp"]),
        mesh=mesh,
        in_specs=(spec, spec, spec, spec, P()),
        out_specs=(spec, P(("group", "dp"), None, None)),
        check_vma=False,
    )
```
